32 devices in a mesh: vol: 2 (over y), space: 16 (over z, x, core).
Axes of the slice: x: 2, y: 2, z: 4, core: 2. Of those that a mesh axis runs over, the one named last changes fastest.
Arguments:
- volume: bfloat16 [2, 32, 64, 8, 128], P('vol', None, 'space'), may hold values from -80 to 80
- conv_weight: bfloat16 [32, 32, 3, 3, 3], replicated, may hold values from -0.21875 to 0.21875
- conv_bias: float32 [32], replicated, may hold values from -3 to 3
- basis: float32 [864, 864], replicated, may hold values from -3 to 3
- damping: float32 [1], replicated, may hold values from 0.5 to 2
Outputs:
- projected: float32 [864, 864], P('vol')
The draws below stay inside these ranges and needn't reach their ends.
All inputs are finite; a program needn't handle non-finite values.
Results may differ from the reference program's by a relative error of at most 0.0019.
Values may be sent and summed in bfloat16 or wider, within the bound.
A program may use at most 64 MiB of HBM per device.

```python
import math
import jax
import jax.numpy as jnp
from jax import lax

C = 32
SY = 8
SZ = 128
SLABS = 2
NX = 64
GRAM_W = 864
PATCHES = 2048


def draw_volume(key, part):
    key_base = jax.random.fold_in(key, 11)
    key_one, key_two, key_three = jax.random.split(key_base, 3)
    full_shape = (SLABS, C, NX, SY, SZ)
    channel_scale = jnp.exp(jax.random.uniform(key_two, (SLABS, C, 1, 1, 1), jnp.float32, math.log(0.3), math.log(3.0)))
    plane_scale = jnp.exp(jax.random.uniform(key_three, (SLABS, 1, NX, 1, 1), jnp.float32, math.log(0.5), math.log(2.0)))
    slab_ramp = (1.8 ** (jnp.arange(SLABS, dtype=jnp.float32) / max(SLABS - 1, 1))).reshape(SLABS, 1, 1, 1, 1)
    plane_ramp = (1.8 ** (jnp.arange(NX, dtype=jnp.float32) / NX)).reshape(1, 1, NX, 1, 1)
    values = jnp.clip(jax.random.normal(key_one, full_shape, jnp.float32), -4.0, 4.0)
    return (values * channel_scale * plane_scale * slab_ramp * plane_ramp).astype(jnp.bfloat16)


def scatter_about(own_key, extent, width, reach, held_as=jnp.bfloat16):
    values = width * jax.random.normal(own_key, extent, jnp.float32)
    return jnp.clip(values, min=-reach, max=reach).astype(held_as)


def setup_inputs(seed: int = 0) -> dict:
    key_of = jax.random.split(jax.random.key(seed), 6)
    volume = draw_volume(jax.random.fold_in(key_of[5], 71), 0)
    conv_weight = scatter_about(key_of[1], (C, C, 3, 3, 3), (27 * C) ** -0.5, 0.21875)
    conv_bias = scatter_about(key_of[2], (C,), 0.5, 3.0, jnp.float32)
    basis = scatter_about(key_of[3], (GRAM_W, GRAM_W), 0.5, 3.0, jnp.float32)
    damping = jnp.clip(jnp.exp(jax.random.uniform(key_of[4], (1,), jnp.float32, math.log(0.5), math.log(2.0))), 0.5, 2.0)
    return dict(volume=volume, conv_weight=conv_weight, conv_bias=conv_bias, basis=basis, damping=damping)


def extract_patches(activated):
    chans, planes, rows_y, cols_z = activated.shape
    viewed = activated.reshape(chans, planes // 4, 4, rows_y // 4, 4, cols_z // 4, 4)[:, :, 1:, :, 1:, :, 1:]
    viewed = viewed.transpose(0, 2, 4, 6, 1, 3, 5)
    return viewed.reshape(chans * 27, -1)


def reference(volume, conv_weight, conv_bias, basis, damping):
    def accumulate(carry, volume_slab):
        conv_out = lax.conv_general_dilated(volume_slab[None], conv_weight, (1, 1, 1), [(1, 1), (1, 1), (1, 1)],
                                            dimension_numbers=("NCDHW", "OIDHW", "NCDHW"),
                                            preferred_element_type=jnp.float32)[0]
        activated = jnp.maximum(conv_out + conv_bias[:, None, None, None], 0.0).astype(jnp.bfloat16)
        patch_cols = extract_patches(activated)
        return carry + jnp.dot(patch_cols, patch_cols.T, preferred_element_type=jnp.float32), None

    gram, unused = lax.scan(accumulate, jnp.zeros((GRAM_W, GRAM_W), jnp.float32), volume)
    normed = gram / PATCHES
    mean_diag = jnp.trace(gram) / PATCHES / GRAM_W
    product = jnp.dot(normed, basis, precision=lax.Precision.HIGHEST, preferred_element_type=jnp.float32)
    return product + damping[0] * mean_diag * basis
```

```python
import functools

import jax
import jax.numpy as jnp
from jax import lax
from jax.experimental import pallas as pl
from jax.experimental.pallas import tpu as pltpu
from jax.sharding import PartitionSpec as P

MESH = pl.DeviceIdType.MESH
GATHER_LIMIT = 8 << 20


def shifted(block, axis, distance):
    devices = range(lax.axis_size(axis))
    route = [(i - distance, i) for i in devices if i - distance in devices]
    return lax.ppermute(block, axis, route)


def split_patches(activated):
    chans, planes, rows_y, cols_z = activated.shape
    return activated.reshape(chans, planes // 4, 4, rows_y // 4, 4, cols_z // 4, 4)[
        :, :, 1:, :, 1:, :, 1:
    ]


def conv_block(volume, conv_weight, conv_bias):
    local_block = volume[0]
    from_above = shifted(local_block[:, 0:1], "space", -1)
    zero_plane = jnp.zeros_like(from_above)
    stacked = jnp.concatenate([zero_plane, local_block, from_above], axis=1)
    conv_out = lax.conv_general_dilated(
        stacked[None],
        conv_weight,
        (1, 1, 1),
        [(0, 0), (1, 1), (1, 1)],
        dimension_numbers=("NCDHW", "OIDHW", "NCDHW"),
        preferred_element_type=jnp.float32,
    )[0]
    return jnp.maximum(conv_out + conv_bias[:, None, None, None], 0.0).astype(jnp.bfloat16)


def body_collective(volume, conv_weight, conv_bias, basis, damping):
    viewed = split_patches(conv_block(volume, conv_weight, conv_bias))
    patch_cols = viewed.transpose(0, 2, 4, 6, 1, 3, 5).reshape(viewed.shape[0] * 27, -1)
    local_gram = jnp.dot(patch_cols, patch_cols.T, preferred_element_type=jnp.float32)
    gram_width = local_gram.shape[0]
    total_patches = patch_cols.shape[1] * lax.axis_size("space") * lax.axis_size("vol")
    panel_rows = gram_width // lax.axis_size("vol")
    row_start = lax.axis_index("vol") * panel_rows
    partial_rows = lax.psum_scatter(
        local_gram.astype(jnp.bfloat16), "vol", scatter_dimension=0, tiled=True
    ).astype(jnp.float32)
    row_panel = lax.psum(partial_rows, "space")
    diag_block = lax.dynamic_slice_in_dim(row_panel, row_start, panel_rows, 1)
    trace_value = lax.psum(jnp.trace(diag_block), "vol")
    normed_panel = row_panel / total_patches
    mean_diagonal = trace_value / total_patches / gram_width
    basis_rows = lax.dynamic_slice_in_dim(basis, row_start, panel_rows, 0)
    product = jnp.dot(
        normed_panel, basis, precision=lax.Precision.HIGHEST, preferred_element_type=jnp.float32
    )
    return product + damping[0] * mean_diagonal * basis_rows


def gather_kernel(
    nz, total, own_ref, basis_hbm, damping_ref, out_ref,
    buf, acc, square, basis_f32, basis_hi, basis_lo,
    basis_sem, z_send, x_send, y_send, a_send, b_send, c_send,
    z_recv, x_recv, y_recv, a_recv, b_recv, c_recv,
):
    vol = lax.axis_index("vol")
    space = lax.axis_index("space")
    z = space // 4
    here = (vol, space)
    core_peer = (vol, space + 1 - 2 * lax.rem(space, 2))
    x_peer = (vol, space + 2 - 4 * lax.rem(space // 2, 2))
    y_peer = (1 - vol, space)
    up_peer, down_peer = (vol, space + 4), (vol, space - 4)
    patches, padded = own_ref.shape
    half = patches // 2
    panel, width = out_ref.shape

    basis_copy = pltpu.make_async_copy(basis_hbm, basis_f32, basis_sem)
    basis_copy.start()

    barrier = pltpu.get_barrier_semaphore()
    for peer in (core_peer, x_peer, y_peer):
        pl.semaphore_signal(barrier, inc=1, device_id=peer, device_id_type=MESH)

    @pl.when(z + 1 < nz)
    def _():
        pl.semaphore_signal(barrier, inc=1, device_id=up_peer, device_id_type=MESH)

    @pl.when(z > 0)
    def _():
        pl.semaphore_signal(barrier, inc=1, device_id=down_peer, device_id_type=MESH)

    buf[0, 0, z] = own_ref[...]
    edges = jnp.where(z > 0, 1, 0) + jnp.where(z + 1 < nz, 1, 0)
    pl.semaphore_wait(barrier, 3 + edges)

    def remote(src, dst, send, recv, peer):
        return pltpu.make_async_remote_copy(
            src_ref=src, dst_ref=dst, send_sem=send, recv_sem=recv,
            device_id=peer, device_id_type=MESH,
        )

    def z_copy(k, peer, way):
        return remote(buf.at[0, 0, k], buf.at[0, 0, k], z_send.at[way, k], z_recv.at[k], peer)

    def x_copy(k):
        return remote(buf.at[0, 0, k], buf.at[0, 1, k], x_send.at[k], x_recv.at[k], x_peer)

    def y_copy(k):
        return remote(buf.at[0, 0, k], buf.at[0, 2, k], y_send.at[k], y_recv.at[k], y_peer)

    def a_copy(k):
        rows = pl.ds(0, half)
        return remote(
            buf.at[0, 1, k, rows], buf.at[0, 3, k, rows], a_send.at[k], a_recv.at[k], y_peer
        )

    def b_copy(k):
        rows = pl.ds(half, half)
        return remote(
            buf.at[0, 2, k, rows], buf.at[0, 3, k, rows], b_send.at[k], b_recv.at[k], x_peer
        )

    def c_copy(q, k):
        return remote(
            buf.at[0, q, k], buf.at[1, q, k], c_send.at[q, k], c_recv.at[q, k], core_peer
        )

    def spread(k):
        x_copy(k).start()
        y_copy(k).start()
        c_copy(0, k).start()

    def relay(k):
        x_copy(k).wait_recv()
        a_copy(k).start()
        c_copy(1, k).start()
        y_copy(k).wait_recv()
        b_copy(k).start()
        c_copy(2, k).start()

    def finish(k):
        a_copy(k).wait_recv()
        b_copy(k).wait_recv()
        c_copy(3, k).start()

    def both(s, action):
        if s == 0:
            action(z)
            return
        pl.when(z >= s)(lambda: action(z - s))
        pl.when(z + s < nz)(lambda: action(z + s))

    def gram(c, q):
        block = buf[c, q].reshape(nz * patches, padded)
        turned = block.T
        wide = block.astype(jnp.float32)
        sums = jnp.sum((wide * wide).reshape(-1, 8, padded), axis=0)
        rows = jnp.where(vol == 0, turned[:panel], turned[panel : 2 * panel])
        term = jnp.dot(rows, block, preferred_element_type=jnp.float32)
        if c == 0 and q == 0:
            acc[...] = term
            square[...] = sums
        else:
            acc[...] += term
            square[...] += sums

    pl.when(z + 1 < nz)(lambda: z_copy(z, up_peer, 0).start())
    pl.when(z > 0)(lambda: z_copy(z, down_peer, 1).start())
    spread(z)

    basis_copy.wait()
    basis_hi[...] = basis_f32[...].astype(jnp.bfloat16)
    basis_lo[...] = (basis_f32[...] - basis_hi[...].astype(jnp.float32)).astype(jnp.bfloat16)

    for s in range(1, nz):
        @pl.when(z >= s)
        def _():
            k = z - s
            z_copy(k, up_peer, 0).wait_recv()
            pl.when(z + 1 < nz)(lambda: z_copy(k, up_peer, 0).start())
            spread(k)

        @pl.when(z + s < nz)
        def _():
            k = z + s
            z_copy(k, down_peer, 1).wait_recv()
            pl.when(z > 0)(lambda: z_copy(k, down_peer, 1).start())
            spread(k)

        both(s - 1, relay)
    gram(0, 0)
    both(nz - 1, relay)
    for s in range(nz):
        both(s, finish)
    for q in range(4):
        if q > 0:
            gram(0, q)
        for k in range(nz):
            c_copy(q, k).wait_recv()
        gram(1, q)

    scale = 1.0 / total
    mean_diag = jnp.sum(square[...]) * (scale / width)
    value = acc[:, :width]
    high = value.astype(jnp.bfloat16)
    low = (value - high.astype(jnp.float32)).astype(jnp.bfloat16)
    product = jnp.dot(high, basis_hi[...], preferred_element_type=jnp.float32)
    product += jnp.dot(high, basis_lo[...], preferred_element_type=jnp.float32)
    product += jnp.dot(low, basis_hi[...], preferred_element_type=jnp.float32)
    basis_rows = basis_f32[pl.ds(pl.multiple_of(vol * panel, 16), panel), :]
    out_ref[...] = product * scale + (damping_ref[0] * mean_diag) * basis_rows

    for k in range(nz):
        pl.when((z + 1 < nz) & (k <= z))(lambda: z_copy(k, up_peer, 0).wait_send())
        pl.when((z > 0) & (k >= z))(lambda: z_copy(k, down_peer, 1).wait_send())
        x_copy(k).wait_send()
        y_copy(k).wait_send()
        a_copy(k).wait_send()
        b_copy(k).wait_send()
        for q in range(4):
            c_copy(q, k).wait_send()


def body_gather(volume, conv_weight, conv_bias, basis, damping):
    viewed = split_patches(conv_block(volume, conv_weight, conv_bias))
    width = viewed.shape[0] * 27
    own = viewed.transpose(1, 3, 5, 0, 2, 4, 6).reshape(-1, width)
    patches = own.shape[0]
    padded = -(-width // 128) * 128
    own = jnp.pad(own, ((0, 0), (0, padded - width)))
    space = lax.axis_size("space")
    nz = space // 4
    panel = width // lax.axis_size("vol")
    total = patches * space * lax.axis_size("vol")
    dma = pltpu.SemaphoreType.DMA
    return pl.pallas_call(
        functools.partial(gather_kernel, nz, total),
        out_shape=jax.ShapeDtypeStruct((panel, width), jnp.float32),
        in_specs=[
            pl.BlockSpec(memory_space=pltpu.VMEM),
            pl.BlockSpec(memory_space=pl.ANY),
            pl.BlockSpec(memory_space=pltpu.SMEM),
        ],
        out_specs=pl.BlockSpec(memory_space=pltpu.VMEM),
        scratch_shapes=[
            pltpu.VMEM((2, 4, nz, patches, padded), jnp.bfloat16),
            pltpu.VMEM((panel, padded), jnp.float32),
            pltpu.VMEM((8, padded), jnp.float32),
            pltpu.VMEM((width, width), jnp.float32),
            pltpu.VMEM((width, width), jnp.bfloat16),
            pltpu.VMEM((width, width), jnp.bfloat16),
            dma,
            dma((2, nz)), dma((nz,)), dma((nz,)), dma((nz,)), dma((nz,)), dma((4, nz)),
            dma((nz,)), dma((nz,)), dma((nz,)), dma((nz,)), dma((nz,)), dma((4, nz)),
        ],
        compiler_params=pltpu.CompilerParams(
            collective_id=0, has_side_effects=True, vmem_limit_bytes=48 << 20
        ),
    )(own, basis, damping)


def body(volume, conv_weight, conv_bias, basis, damping):
    vol, space = lax.axis_size("vol"), lax.axis_size("space")
    cells = volume.shape[2] * volume.shape[3] * volume.shape[4]
    gathered = 2 * volume.shape[1] * 27 * (cells // 64) * vol * space
    if vol == 2 and space % 4 == 0 and gathered <= GATHER_LIMIT:
        return body_gather(volume, conv_weight, conv_bias, basis, damping)
    return body_collective(volume, conv_weight, conv_bias, basis, damping)


def solution(mesh):
    in_specs = (P("vol", None, "space", None, None), P(), P(), P(), P())
    out_specs = P("vol", None)
    return jax.shard_map(body, mesh=mesh, in_specs=in_specs, out_specs=out_specs, check_vma=False)
```

```python
import functools

import jax
import jax.numpy as jnp
from jax import lax
from jax.experimental import pallas as pl
from jax.experimental.pallas import tpu as pltpu
from jax.sharding import PartitionSpec as P

MESH = pl.DeviceIdType.MESH
GATHER_LIMIT = 8 << 20


def shifted(block, axis, distance):
    devices = range(lax.axis_size(axis))
    route = [(i - distance, i) for i in devices if i - distance in devices]
    return lax.ppermute(block, axis, route)


def split_patches(activated):
    chans, planes, rows_y, cols_z = activated.shape
    return activated.reshape(chans, planes // 4, 4, rows_y // 4, 4, cols_z // 4, 4)[
        :, :, 1:, :, 1:, :, 1:
    ]


def conv_block(volume, conv_weight, conv_bias):
    local_block = volume[0]
    from_above = shifted(local_block[:, 0:1], "space", -1)
    zero_plane = jnp.zeros_like(from_above)
    stacked = jnp.concatenate([zero_plane, local_block, from_above], axis=1)
    conv_out = lax.conv_general_dilated(
        stacked[None],
        conv_weight,
        (1, 1, 1),
        [(0, 0), (1, 1), (1, 1)],
        dimension_numbers=("NCDHW", "OIDHW", "NCDHW"),
        preferred_element_type=jnp.float32,
    )[0]
    return jnp.maximum(conv_out + conv_bias[:, None, None, None], 0.0).astype(jnp.bfloat16)


def body_collective(volume, conv_weight, conv_bias, basis, damping):
    viewed = split_patches(conv_block(volume, conv_weight, conv_bias))
    patch_cols = viewed.transpose(0, 2, 4, 6, 1, 3, 5).reshape(viewed.shape[0] * 27, -1)
    local_gram = jnp.dot(patch_cols, patch_cols.T, preferred_element_type=jnp.float32)
    gram_width = local_gram.shape[0]
    total_patches = patch_cols.shape[1] * lax.axis_size("space") * lax.axis_size("vol")
    panel_rows = gram_width // lax.axis_size("vol")
    row_start = lax.axis_index("vol") * panel_rows
    partial_rows = lax.psum_scatter(
        local_gram.astype(jnp.bfloat16), "vol", scatter_dimension=0, tiled=True
    ).astype(jnp.float32)
    row_panel = lax.psum(partial_rows, "space")
    diag_block = lax.dynamic_slice_in_dim(row_panel, row_start, panel_rows, 1)
    trace_value = lax.psum(jnp.trace(diag_block), "vol")
    normed_panel = row_panel / total_patches
    mean_diagonal = trace_value / total_patches / gram_width
    basis_rows = lax.dynamic_slice_in_dim(basis, row_start, panel_rows, 0)
    product = jnp.dot(
        normed_panel, basis, precision=lax.Precision.HIGHEST, preferred_element_type=jnp.float32
    )
    return product + damping[0] * mean_diagonal * basis_rows


def wait_halo(present, halo_copy, halo):
    @pl.when(present)
    def _():
        halo_copy().wait_recv()

    @pl.when(jnp.logical_not(present))
    def _():
        halo[...] = jnp.zeros_like(halo)


def own_patches(
    cells_ref, weight_ref, bias_ref, halo, taps, partial, active, padded, wait
):
    planes, rows_y, chans, cols_z = cells_ref.shape
    out_rows = [y for y in range(rows_y) if y % 4]
    lane = lax.broadcasted_iota(jnp.int32, (rows_y * chans, cols_z), 1)

    def plane(p, cells):
        wide = cells.astype(jnp.float32).reshape(rows_y * chans, cols_z)
        left = jnp.where(lane == 0, 0.0, pltpu.roll(wide, 1, 1))
        right = jnp.where(lane == cols_z - 1, 0.0, pltpu.roll(wide, cols_z - 1, 1))
        for d, moved in enumerate((left, wide, right)):
            taps[0:rows_y, d] = moved.astype(jnp.bfloat16).reshape(rows_y, chans, cols_z)
        taps[rows_y] = jnp.zeros_like(taps[rows_y])
        for n, y in enumerate(out_rows):
            window = taps[y - 1 : y + 2].reshape(9 * chans, cols_z)
            partial[p, n] = jnp.dot(
                weight_ref[...], window, preferred_element_type=jnp.float32
            )

    for p in range(planes):
        plane(p, cells_ref[p])

    source = lax.broadcasted_iota(jnp.int32, (9 * chans, padded), 0)
    target = lax.broadcasted_iota(jnp.int32, (9 * chans, padded), 1)
    target -= (source % chans) * 27 + (source // chans) * 3
    order = [jnp.where(target == c, 1.0, 0.0).astype(jnp.bfloat16) for c in range(3)]
    ks = cols_z // 4
    row = lax.broadcasted_iota(jnp.int32, (3 * ks, cols_z), 0)
    col = lax.broadcasted_iota(jnp.int32, (3 * ks, cols_z), 1)
    pick = jnp.where(col == 4 * (row % ks) + row // ks + 1, 1.0, 0.0).astype(jnp.bfloat16)

    wait()
    plane(planes, halo[...])

    picked = []
    for j in range(rows_y // 4):
        for a in range(3):
            for b in range(3):
                n = 3 * j + b
                value = partial[a, n, 0:chans] + partial[a + 1, n, chans : 2 * chans]
                value += partial[a + 2, n, 2 * chans : 3 * chans]
                value = jnp.maximum(value + bias_ref[...], 0.0).astype(jnp.bfloat16)
                active[(3 * a + b) * chans : (3 * a + b + 1) * chans] = value
        picked.append(
            lax.dot_general(
                pick, active[...], (((1,), (1,)), ((), ())), preferred_element_type=jnp.float32
            ).astype(jnp.bfloat16)
        )
    total = None
    for c in range(3):
        part = jnp.concatenate([x[c * ks : (c + 1) * ks] for x in picked], axis=0)
        term = jnp.dot(part, order[c], preferred_element_type=jnp.float32)
        total = term if total is None else total + term
    return total.astype(jnp.bfloat16)


def gather_kernel(
    nz, total, cells_ref, weight_ref, bias_ref, basis_hbm, damping_ref, out_ref,
    halo, taps, partial, active, buf, acc, square, basis_f32, basis_hi, basis_lo,
    basis_sem, halo_send, halo_recv, z_send, x_send, y_send, a_send, b_send, c_send,
    z_recv, x_recv, y_recv, a_recv, b_recv, c_recv,
):
    vol = lax.axis_index("vol")
    space = lax.axis_index("space")
    z = space // 4
    here = (vol, space)
    core_peer = (vol, space + 1 - 2 * lax.rem(space, 2))
    x_peer = (vol, space + 2 - 4 * lax.rem(space // 2, 2))
    y_peer = (1 - vol, space)
    up_peer, down_peer = (vol, space + 4), (vol, space - 4)
    patches, padded = buf.shape[3:]
    ends = lax.axis_size("space")
    half = patches // 2
    panel, width = out_ref.shape

    basis_copy = pltpu.make_async_copy(basis_hbm, basis_f32, basis_sem)
    basis_copy.start()

    barrier = pltpu.get_barrier_semaphore()
    for peer in (core_peer, x_peer, y_peer):
        pl.semaphore_signal(barrier, inc=1, device_id=peer, device_id_type=MESH)

    @pl.when(z + 1 < nz)
    def _():
        pl.semaphore_signal(barrier, inc=1, device_id=up_peer, device_id_type=MESH)

    @pl.when(z > 0)
    def _():
        pl.semaphore_signal(barrier, inc=1, device_id=down_peer, device_id_type=MESH)

    @pl.when(space > 0)
    def _():
        pl.semaphore_signal(barrier, inc=1, device_id=(vol, space - 1), device_id_type=MESH)

    @pl.when(space + 1 < ends)
    def _():
        pl.semaphore_signal(barrier, inc=1, device_id=(vol, space + 1), device_id_type=MESH)

    edges = jnp.where(z > 0, 1, 0) + jnp.where(z + 1 < nz, 1, 0)
    edges += jnp.where(space > 0, 1, 0) + jnp.where(space + 1 < ends, 1, 0)
    pl.semaphore_wait(barrier, 3 + edges)

    def remote(src, dst, send, recv, peer):
        return pltpu.make_async_remote_copy(
            src_ref=src, dst_ref=dst, send_sem=send, recv_sem=recv,
            device_id=peer, device_id_type=MESH,
        )

    def halo_copy():
        return remote(cells_ref.at[0], halo, halo_send, halo_recv, (vol, space - 1))

    pl.when(space > 0)(lambda: halo_copy().start())
    buf[0, 0, z] = own_patches(
        cells_ref, weight_ref, bias_ref, halo, taps, partial, active, padded,
        lambda: wait_halo(space + 1 < ends, halo_copy, halo),
    )

    def z_copy(k, peer, way):
        return remote(buf.at[0, 0, k], buf.at[0, 0, k], z_send.at[way, k], z_recv.at[k], peer)

    def x_copy(k):
        return remote(buf.at[0, 0, k], buf.at[0, 1, k], x_send.at[k], x_recv.at[k], x_peer)

    def y_copy(k):
        return remote(buf.at[0, 0, k], buf.at[0, 2, k], y_send.at[k], y_recv.at[k], y_peer)

    def a_copy(k):
        rows = pl.ds(0, half)
        return remote(
            buf.at[0, 1, k, rows], buf.at[0, 3, k, rows], a_send.at[k], a_recv.at[k], y_peer
        )

    def b_copy(k):
        rows = pl.ds(half, half)
        return remote(
            buf.at[0, 2, k, rows], buf.at[0, 3, k, rows], b_send.at[k], b_recv.at[k], x_peer
        )

    def c_copy(q, k):
        return remote(
            buf.at[0, q, k], buf.at[1, q, k], c_send.at[q, k], c_recv.at[q, k], core_peer
        )

    def spread(k):
        x_copy(k).start()
        y_copy(k).start()
        c_copy(0, k).start()

    def relay(k):
        x_copy(k).wait_recv()
        a_copy(k).start()
        c_copy(1, k).start()
        y_copy(k).wait_recv()
        b_copy(k).start()
        c_copy(2, k).start()

    def finish(k):
        a_copy(k).wait_recv()
        b_copy(k).wait_recv()
        c_copy(3, k).start()

    def both(s, action):
        if s == 0:
            action(z)
            return
        pl.when(z >= s)(lambda: action(z - s))
        pl.when(z + s < nz)(lambda: action(z + s))

    def gram(c, q):
        block = buf[c, q].reshape(nz * patches, padded)
        turned = block.T
        wide = block.astype(jnp.float32)
        sums = jnp.sum((wide * wide).reshape(-1, 8, padded), axis=0)
        rows = jnp.where(vol == 0, turned[:panel], turned[panel : 2 * panel])
        term = jnp.dot(rows, block, preferred_element_type=jnp.float32)
        if c == 0 and q == 0:
            acc[...] = term
            square[...] = sums
        else:
            acc[...] += term
            square[...] += sums

    pl.when(z + 1 < nz)(lambda: z_copy(z, up_peer, 0).start())
    pl.when(z > 0)(lambda: z_copy(z, down_peer, 1).start())
    spread(z)

    basis_copy.wait()
    basis_hi[...] = basis_f32[...].astype(jnp.bfloat16)
    basis_lo[...] = (basis_f32[...] - basis_hi[...].astype(jnp.float32)).astype(jnp.bfloat16)

    for s in range(1, nz):
        @pl.when(z >= s)
        def _():
            k = z - s
            z_copy(k, up_peer, 0).wait_recv()
            pl.when(z + 1 < nz)(lambda: z_copy(k, up_peer, 0).start())
            spread(k)

        @pl.when(z + s < nz)
        def _():
            k = z + s
            z_copy(k, down_peer, 1).wait_recv()
            pl.when(z > 0)(lambda: z_copy(k, down_peer, 1).start())
            spread(k)

        both(s - 1, relay)
    gram(0, 0)
    both(nz - 1, relay)
    for s in range(nz):
        both(s, finish)
    for q in range(4):
        if q > 0:
            gram(0, q)
        for k in range(nz):
            c_copy(q, k).wait_recv()
        gram(1, q)

    scale = 1.0 / total
    mean_diag = jnp.sum(square[...]) * (scale / width)
    value = acc[:, :width]
    high = value.astype(jnp.bfloat16)
    low = (value - high.astype(jnp.float32)).astype(jnp.bfloat16)
    product = jnp.dot(high, basis_hi[...], preferred_element_type=jnp.float32)
    product += jnp.dot(high, basis_lo[...], preferred_element_type=jnp.float32)
    product += jnp.dot(low, basis_hi[...], preferred_element_type=jnp.float32)
    basis_rows = basis_f32[pl.ds(pl.multiple_of(vol * panel, 16), panel), :]
    out_ref[...] = product * scale + (damping_ref[0] * mean_diag) * basis_rows

    pl.when(space > 0)(lambda: halo_copy().wait_send())
    for k in range(nz):
        pl.when((z + 1 < nz) & (k <= z))(lambda: z_copy(k, up_peer, 0).wait_send())
        pl.when((z > 0) & (k >= z))(lambda: z_copy(k, down_peer, 1).wait_send())
        x_copy(k).wait_send()
        y_copy(k).wait_send()
        a_copy(k).wait_send()
        b_copy(k).wait_send()
        for q in range(4):
            c_copy(q, k).wait_send()


def body_gather(volume, conv_weight, conv_bias, basis, damping):
    chans, planes, rows_y, cols_z = volume.shape[1:]
    width = chans * 27
    patches = (planes // 4) * (rows_y // 4) * (cols_z // 4)
    cells = volume[0].transpose(1, 2, 0, 3)
    weight = conv_weight.transpose(2, 0, 3, 4, 1).reshape(3 * chans, 9 * chans)
    padded = -(-width // 128) * 128
    space = lax.axis_size("space")
    nz = space // 4
    panel = width // lax.axis_size("vol")
    total = patches * space * lax.axis_size("vol")
    dma = pltpu.SemaphoreType.DMA
    return pl.pallas_call(
        functools.partial(gather_kernel, nz, total),
        out_shape=jax.ShapeDtypeStruct((panel, width), jnp.float32),
        in_specs=[
            pl.BlockSpec(memory_space=pltpu.VMEM),
            pl.BlockSpec(memory_space=pltpu.VMEM),
            pl.BlockSpec(memory_space=pltpu.VMEM),
            pl.BlockSpec(memory_space=pltpu.HBM),
            pl.BlockSpec(memory_space=pltpu.SMEM),
        ],
        out_specs=pl.BlockSpec(memory_space=pltpu.VMEM),
        scratch_shapes=[
            pltpu.VMEM((rows_y, chans, cols_z), jnp.bfloat16),
            pltpu.VMEM((rows_y + 1, 3, chans, cols_z), jnp.bfloat16),
            pltpu.VMEM((planes + 1, 3 * rows_y // 4, 3 * chans, cols_z), jnp.float32),
            pltpu.VMEM((9 * chans, cols_z), jnp.bfloat16),
            pltpu.VMEM((2, 4, nz, patches, padded), jnp.bfloat16),
            pltpu.VMEM((panel, padded), jnp.float32),
            pltpu.VMEM((8, padded), jnp.float32),
            pltpu.VMEM((width, width), jnp.float32),
            pltpu.VMEM((width, width), jnp.bfloat16),
            pltpu.VMEM((width, width), jnp.bfloat16),
            dma, dma, dma,
            dma((2, nz)), dma((nz,)), dma((nz,)), dma((nz,)), dma((nz,)), dma((4, nz)),
            dma((nz,)), dma((nz,)), dma((nz,)), dma((nz,)), dma((nz,)), dma((4, nz)),
        ],
        compiler_params=pltpu.CompilerParams(
            collective_id=0, has_side_effects=True, vmem_limit_bytes=48 << 20
        ),
    )(cells, weight, conv_bias[:, None], basis, damping)


def body(volume, conv_weight, conv_bias, basis, damping):
    vol, space = lax.axis_size("vol"), lax.axis_size("space")
    cells = volume.shape[2] * volume.shape[3] * volume.shape[4]
    gathered = 2 * volume.shape[1] * 27 * (cells // 64) * vol * space
    one_plane = volume.shape[2] == 4 and volume.shape[4] % 128 == 0
    if one_plane and vol == 2 and space % 4 == 0 and gathered <= GATHER_LIMIT:
        return body_gather(volume, conv_weight, conv_bias, basis, damping)
    return body_collective(volume, conv_weight, conv_bias, basis, damping)


def solution(mesh):
    in_specs = (P("vol", None, "space", None, None), P(), P(), P(), P())
    out_specs = P("vol", None)
    return jax.shard_map(body, mesh=mesh, in_specs=in_specs, out_specs=out_specs, check_vma=False)
```

```python
import functools

import jax
import jax.numpy as jnp
from jax import lax
from jax.experimental import pallas as pl
from jax.experimental.pallas import tpu as pltpu
from jax.sharding import PartitionSpec as P

MESH = pl.DeviceIdType.MESH
GATHER_LIMIT = 8 << 20


def shifted(block, axis, distance):
    devices = range(lax.axis_size(axis))
    route = [(i - distance, i) for i in devices if i - distance in devices]
    return lax.ppermute(block, axis, route)


def split_patches(activated):
    chans, planes, rows_y, cols_z = activated.shape
    return activated.reshape(chans, planes // 4, 4, rows_y // 4, 4, cols_z // 4, 4)[
        :, :, 1:, :, 1:, :, 1:
    ]


def conv_block(volume, conv_weight, conv_bias):
    local_block = volume[0]
    from_above = shifted(local_block[:, 0:1], "space", -1)
    zero_plane = jnp.zeros_like(from_above)
    stacked = jnp.concatenate([zero_plane, local_block, from_above], axis=1)
    conv_out = lax.conv_general_dilated(
        stacked[None],
        conv_weight,
        (1, 1, 1),
        [(0, 0), (1, 1), (1, 1)],
        dimension_numbers=("NCDHW", "OIDHW", "NCDHW"),
        preferred_element_type=jnp.float32,
    )[0]
    return jnp.maximum(conv_out + conv_bias[:, None, None, None], 0.0).astype(jnp.bfloat16)


def body_collective(volume, conv_weight, conv_bias, basis, damping):
    viewed = split_patches(conv_block(volume, conv_weight, conv_bias))
    patch_cols = viewed.transpose(0, 2, 4, 6, 1, 3, 5).reshape(viewed.shape[0] * 27, -1)
    local_gram = jnp.dot(patch_cols, patch_cols.T, preferred_element_type=jnp.float32)
    gram_width = local_gram.shape[0]
    total_patches = patch_cols.shape[1] * lax.axis_size("space") * lax.axis_size("vol")
    panel_rows = gram_width // lax.axis_size("vol")
    row_start = lax.axis_index("vol") * panel_rows
    partial_rows = lax.psum_scatter(
        local_gram.astype(jnp.bfloat16), "vol", scatter_dimension=0, tiled=True
    ).astype(jnp.float32)
    row_panel = lax.psum(partial_rows, "space")
    diag_block = lax.dynamic_slice_in_dim(row_panel, row_start, panel_rows, 1)
    trace_value = lax.psum(jnp.trace(diag_block), "vol")
    normed_panel = row_panel / total_patches
    mean_diagonal = trace_value / total_patches / gram_width
    basis_rows = lax.dynamic_slice_in_dim(basis, row_start, panel_rows, 0)
    product = jnp.dot(
        normed_panel, basis, precision=lax.Precision.HIGHEST, preferred_element_type=jnp.float32
    )
    return product + damping[0] * mean_diagonal * basis_rows


def wait_halo(present, halo_copy, halo):
    @pl.when(present)
    def _():
        halo_copy().wait_recv()

    @pl.when(jnp.logical_not(present))
    def _():
        halo[...] = jnp.zeros_like(halo)


def own_patches(
    cells_ref, weight_ref, bias_ref, halo, weights, taps, partial, active, padded, wait
):
    planes, rows_y, chans, cols_z = cells_ref.shape
    out_rows = [y for y in range(rows_y) if y % 4]
    lane = lax.broadcasted_iota(jnp.int32, (rows_y * chans, cols_z), 1)

    for d in range(3):
        weights[d * chans : (d + 1) * chans] = jnp.concatenate(
            [weight_ref[9 * d + t].astype(jnp.float32) for t in range(9)], axis=1
        ).astype(jnp.bfloat16)

    def plane(p, cells):
        wide = cells.astype(jnp.float32).reshape(rows_y * chans, cols_z)
        left = jnp.where(lane == 0, 0.0, pltpu.roll(wide, 1, 1))
        right = jnp.where(lane == cols_z - 1, 0.0, pltpu.roll(wide, cols_z - 1, 1))
        for d, moved in enumerate((left, wide, right)):
            taps[0:rows_y, d] = moved.astype(jnp.bfloat16).reshape(rows_y, chans, cols_z)
        taps[rows_y] = jnp.zeros_like(taps[rows_y])
        for n, y in enumerate(out_rows):
            window = taps[y - 1 : y + 2].reshape(9 * chans, cols_z)
            partial[p, n] = jnp.dot(
                weights[...], window, preferred_element_type=jnp.float32
            )

    for p in range(planes):
        plane(p, cells_ref[p])

    source = lax.broadcasted_iota(jnp.int32, (9 * chans, padded), 0)
    target = lax.broadcasted_iota(jnp.int32, (9 * chans, padded), 1)
    target -= (source % chans) * 27 + (source // chans) * 3
    order = [jnp.where(target == c, 1.0, 0.0).astype(jnp.bfloat16) for c in range(3)]
    ks = cols_z // 4
    row = lax.broadcasted_iota(jnp.int32, (3 * ks, cols_z), 0)
    col = lax.broadcasted_iota(jnp.int32, (3 * ks, cols_z), 1)
    pick = jnp.where(col == 4 * (row % ks) + row // ks + 1, 1.0, 0.0).astype(jnp.bfloat16)

    square = (chans, chans)
    diagonal = lax.broadcasted_iota(jnp.int32, square, 0) == lax.broadcasted_iota(
        jnp.int32, square, 1
    )
    bias = jnp.sum(jnp.where(diagonal, bias_ref[...], 0.0), axis=1, keepdims=True)

    wait()
    plane(planes, halo[...])

    picked = []
    for j in range(rows_y // 4):
        for a in range(3):
            for b in range(3):
                n = 3 * j + b
                value = partial[a, n, 0:chans] + partial[a + 1, n, chans : 2 * chans]
                value += partial[a + 2, n, 2 * chans : 3 * chans]
                value = jnp.maximum(value + bias, 0.0).astype(jnp.bfloat16)
                active[(3 * a + b) * chans : (3 * a + b + 1) * chans] = value
        picked.append(
            lax.dot_general(
                pick, active[...], (((1,), (1,)), ((), ())), preferred_element_type=jnp.float32
            ).astype(jnp.bfloat16)
        )
    total = None
    for c in range(3):
        part = jnp.concatenate([x[c * ks : (c + 1) * ks] for x in picked], axis=0)
        term = jnp.dot(part, order[c], preferred_element_type=jnp.float32)
        total = term if total is None else total + term
    return total.astype(jnp.bfloat16)


def gather_kernel(
    nz, total, cells_ref, weight_ref, bias_ref, basis_hbm, damping_ref, out_ref,
    halo, weights, taps, partial, active, buf, acc, square, basis_f32, basis_hi, basis_lo,
    basis_sem, halo_send, halo_recv, z_send, x_send, y_send, a_send, b_send, c_send,
    z_recv, x_recv, y_recv, a_recv, b_recv, c_recv,
):
    vol = lax.axis_index("vol")
    space = lax.axis_index("space")
    z = space // 4
    here = (vol, space)
    core_peer = (vol, space + 1 - 2 * lax.rem(space, 2))
    x_peer = (vol, space + 2 - 4 * lax.rem(space // 2, 2))
    y_peer = (1 - vol, space)
    up_peer, down_peer = (vol, space + 4), (vol, space - 4)
    patches, padded = buf.shape[3:]
    ends = lax.axis_size("space")
    half = patches // 2
    panel, width = out_ref.shape

    basis_copy = pltpu.make_async_copy(basis_hbm, basis_f32, basis_sem)
    basis_copy.start()

    barrier = pltpu.get_barrier_semaphore()
    for peer in (core_peer, x_peer, y_peer):
        pl.semaphore_signal(barrier, inc=1, device_id=peer, device_id_type=MESH)

    @pl.when(z + 1 < nz)
    def _():
        pl.semaphore_signal(barrier, inc=1, device_id=up_peer, device_id_type=MESH)

    @pl.when(z > 0)
    def _():
        pl.semaphore_signal(barrier, inc=1, device_id=down_peer, device_id_type=MESH)

    @pl.when(space > 0)
    def _():
        pl.semaphore_signal(barrier, inc=1, device_id=(vol, space - 1), device_id_type=MESH)

    @pl.when(space + 1 < ends)
    def _():
        pl.semaphore_signal(barrier, inc=1, device_id=(vol, space + 1), device_id_type=MESH)

    edges = jnp.where(z > 0, 1, 0) + jnp.where(z + 1 < nz, 1, 0)
    edges += jnp.where(space > 0, 1, 0) + jnp.where(space + 1 < ends, 1, 0)
    pl.semaphore_wait(barrier, 3 + edges)

    def remote(src, dst, send, recv, peer):
        return pltpu.make_async_remote_copy(
            src_ref=src, dst_ref=dst, send_sem=send, recv_sem=recv,
            device_id=peer, device_id_type=MESH,
        )

    def halo_copy():
        return remote(cells_ref.at[0], halo, halo_send, halo_recv, (vol, space - 1))

    pl.when(space > 0)(lambda: halo_copy().start())
    buf[0, 0, z] = own_patches(
        cells_ref, weight_ref, bias_ref, halo, weights, taps, partial, active, padded,
        lambda: wait_halo(space + 1 < ends, halo_copy, halo),
    )

    def z_copy(k, peer, way):
        return remote(buf.at[0, 0, k], buf.at[0, 0, k], z_send.at[way, k], z_recv.at[k], peer)

    def x_copy(k):
        return remote(buf.at[0, 0, k], buf.at[0, 1, k], x_send.at[k], x_recv.at[k], x_peer)

    def y_copy(k):
        return remote(buf.at[0, 0, k], buf.at[0, 2, k], y_send.at[k], y_recv.at[k], y_peer)

    def a_copy(k):
        rows = pl.ds(0, half)
        return remote(
            buf.at[0, 1, k, rows], buf.at[0, 3, k, rows], a_send.at[k], a_recv.at[k], y_peer
        )

    def b_copy(k):
        rows = pl.ds(half, half)
        return remote(
            buf.at[0, 2, k, rows], buf.at[0, 3, k, rows], b_send.at[k], b_recv.at[k], x_peer
        )

    def c_copy(q, k):
        return remote(
            buf.at[0, q, k], buf.at[1, q, k], c_send.at[q, k], c_recv.at[q, k], core_peer
        )

    def spread(k):
        x_copy(k).start()
        y_copy(k).start()
        c_copy(0, k).start()

    def relay(k):
        x_copy(k).wait_recv()
        a_copy(k).start()
        c_copy(1, k).start()
        y_copy(k).wait_recv()
        b_copy(k).start()
        c_copy(2, k).start()

    def finish(k):
        a_copy(k).wait_recv()
        b_copy(k).wait_recv()
        c_copy(3, k).start()

    def both(s, action):
        if s == 0:
            action(z)
            return
        pl.when(z >= s)(lambda: action(z - s))
        pl.when(z + s < nz)(lambda: action(z + s))

    def gram(c, q):
        block = buf[c, q].reshape(nz * patches, padded)
        turned = block.T
        wide = block.astype(jnp.float32)
        sums = jnp.sum((wide * wide).reshape(-1, 8, padded), axis=0)
        rows = jnp.where(vol == 0, turned[:panel], turned[panel : 2 * panel])
        term = jnp.dot(rows, block, preferred_element_type=jnp.float32)
        if c == 0 and q == 0:
            acc[...] = term
            square[...] = sums
        else:
            acc[...] += term
            square[...] += sums

    pl.when(z + 1 < nz)(lambda: z_copy(z, up_peer, 0).start())
    pl.when(z > 0)(lambda: z_copy(z, down_peer, 1).start())
    spread(z)

    basis_copy.wait()
    basis_hi[...] = basis_f32[...].astype(jnp.bfloat16)
    basis_lo[...] = (basis_f32[...] - basis_hi[...].astype(jnp.float32)).astype(jnp.bfloat16)

    for s in range(1, nz):
        @pl.when(z >= s)
        def _():
            k = z - s
            z_copy(k, up_peer, 0).wait_recv()
            pl.when(z + 1 < nz)(lambda: z_copy(k, up_peer, 0).start())
            spread(k)

        @pl.when(z + s < nz)
        def _():
            k = z + s
            z_copy(k, down_peer, 1).wait_recv()
            pl.when(z > 0)(lambda: z_copy(k, down_peer, 1).start())
            spread(k)

        both(s - 1, relay)
    both(nz - 1, relay)

    def other_core(q):
        for k in range(nz):
            c_copy(q, k).wait_recv()
        gram(1, q)

    early = [
        lambda: gram(0, 0), lambda: other_core(0), lambda: gram(0, 1),
        lambda: gram(0, 2), lambda: other_core(1), lambda: other_core(2),
    ]
    for s in range(nz):
        share = -(-len(early) // (nz - s))
        for step in early[:share]:
            step()
        early = early[share:]
        both(s, finish)
    gram(0, 3)
    other_core(3)

    scale = 1.0 / total
    mean_diag = jnp.sum(square[...]) * (scale / width)
    value = acc[:, :width]
    high = value.astype(jnp.bfloat16)
    low = (value - high.astype(jnp.float32)).astype(jnp.bfloat16)
    product = jnp.dot(high, basis_hi[...], preferred_element_type=jnp.float32)
    product += jnp.dot(high, basis_lo[...], preferred_element_type=jnp.float32)
    product += jnp.dot(low, basis_hi[...], preferred_element_type=jnp.float32)
    basis_rows = basis_f32[pl.ds(pl.multiple_of(vol * panel, 16), panel), :]
    out_ref[...] = product * scale + (damping_ref[0] * mean_diag) * basis_rows

    pl.when(space > 0)(lambda: halo_copy().wait_send())
    for k in range(nz):
        pl.when((z + 1 < nz) & (k <= z))(lambda: z_copy(k, up_peer, 0).wait_send())
        pl.when((z > 0) & (k >= z))(lambda: z_copy(k, down_peer, 1).wait_send())
        x_copy(k).wait_send()
        y_copy(k).wait_send()
        a_copy(k).wait_send()
        b_copy(k).wait_send()
        for q in range(4):
            c_copy(q, k).wait_send()


def body_gather(volume, conv_weight, conv_bias, basis, damping):
    chans, planes, rows_y, cols_z = volume.shape[1:]
    width = chans * 27
    patches = (planes // 4) * (rows_y // 4) * (cols_z // 4)
    cells = volume[0].transpose(1, 2, 0, 3)
    weight = conv_weight.transpose(2, 3, 4, 0, 1).reshape(27, chans, chans)
    padded = -(-width // 128) * 128
    space = lax.axis_size("space")
    nz = space // 4
    panel = width // lax.axis_size("vol")
    total = patches * space * lax.axis_size("vol")
    dma = pltpu.SemaphoreType.DMA
    return pl.pallas_call(
        functools.partial(gather_kernel, nz, total),
        out_shape=jax.ShapeDtypeStruct((panel, width), jnp.float32),
        in_specs=[
            pl.BlockSpec(memory_space=pltpu.VMEM),
            pl.BlockSpec(memory_space=pltpu.VMEM),
            pl.BlockSpec(memory_space=pltpu.VMEM),
            pl.BlockSpec(memory_space=pltpu.HBM),
            pl.BlockSpec(memory_space=pltpu.SMEM),
        ],
        out_specs=pl.BlockSpec(memory_space=pltpu.VMEM),
        scratch_shapes=[
            pltpu.VMEM((rows_y, chans, cols_z), jnp.bfloat16),
            pltpu.VMEM((3 * chans, 9 * chans), jnp.bfloat16),
            pltpu.VMEM((rows_y + 1, 3, chans, cols_z), jnp.bfloat16),
            pltpu.VMEM((planes + 1, 3 * rows_y // 4, 3 * chans, cols_z), jnp.float32),
            pltpu.VMEM((9 * chans, cols_z), jnp.bfloat16),
            pltpu.VMEM((2, 4, nz, patches, padded), jnp.bfloat16),
            pltpu.VMEM((panel, padded), jnp.float32),
            pltpu.VMEM((8, padded), jnp.float32),
            pltpu.VMEM((width, width), jnp.float32),
            pltpu.VMEM((width, width), jnp.bfloat16),
            pltpu.VMEM((width, width), jnp.bfloat16),
            dma, dma, dma,
            dma((2, nz)), dma((nz,)), dma((nz,)), dma((nz,)), dma((nz,)), dma((4, nz)),
            dma((nz,)), dma((nz,)), dma((nz,)), dma((nz,)), dma((nz,)), dma((4, nz)),
        ],
        compiler_params=pltpu.CompilerParams(
            collective_id=0, has_side_effects=True, vmem_limit_bytes=61 << 20
        ),
    )(cells, weight, conv_bias[None, :], basis, damping)


def body(volume, conv_weight, conv_bias, basis, damping):
    vol, space = lax.axis_size("vol"), lax.axis_size("space")
    cells = volume.shape[2] * volume.shape[3] * volume.shape[4]
    gathered = 2 * volume.shape[1] * 27 * (cells // 64) * vol * space
    one_plane = volume.shape[2] == 4 and volume.shape[4] % 128 == 0
    if one_plane and vol == 2 and space % 4 == 0 and gathered <= GATHER_LIMIT:
        return body_gather(volume, conv_weight, conv_bias, basis, damping)
    return body_collective(volume, conv_weight, conv_bias, basis, damping)


def solution(mesh):
    in_specs = (P("vol", None, "space", None, None), P(), P(), P(), P())
    out_specs = P("vol", None)
    return jax.shard_map(body, mesh=mesh, in_specs=in_specs, out_specs=out_specs, check_vma=False)
```

```python
import functools

import jax
import jax.numpy as jnp
from jax import lax
from jax.experimental import pallas as pl
from jax.experimental.pallas import tpu as pltpu
from jax.sharding import PartitionSpec as P

MESH = pl.DeviceIdType.MESH
GATHER_LIMIT = 8 << 20


def shifted(block, axis, distance):
    devices = range(lax.axis_size(axis))
    route = [(i - distance, i) for i in devices if i - distance in devices]
    return lax.ppermute(block, axis, route)


def split_patches(activated):
    chans, planes, rows_y, cols_z = activated.shape
    return activated.reshape(chans, planes // 4, 4, rows_y // 4, 4, cols_z // 4, 4)[
        :, :, 1:, :, 1:, :, 1:
    ]


def conv_block(volume, conv_weight, conv_bias):
    local_block = volume[0]
    from_above = shifted(local_block[:, 0:1], "space", -1)
    zero_plane = jnp.zeros_like(from_above)
    stacked = jnp.concatenate([zero_plane, local_block, from_above], axis=1)
    conv_out = lax.conv_general_dilated(
        stacked[None],
        conv_weight,
        (1, 1, 1),
        [(0, 0), (1, 1), (1, 1)],
        dimension_numbers=("NCDHW", "OIDHW", "NCDHW"),
        preferred_element_type=jnp.float32,
    )[0]
    return jnp.maximum(conv_out + conv_bias[:, None, None, None], 0.0).astype(jnp.bfloat16)


def body_collective(volume, conv_weight, conv_bias, basis, damping):
    viewed = split_patches(conv_block(volume, conv_weight, conv_bias))
    patch_cols = viewed.transpose(0, 2, 4, 6, 1, 3, 5).reshape(viewed.shape[0] * 27, -1)
    local_gram = jnp.dot(patch_cols, patch_cols.T, preferred_element_type=jnp.float32)
    gram_width = local_gram.shape[0]
    total_patches = patch_cols.shape[1] * lax.axis_size("space") * lax.axis_size("vol")
    panel_rows = gram_width // lax.axis_size("vol")
    row_start = lax.axis_index("vol") * panel_rows
    partial_rows = lax.psum_scatter(
        local_gram.astype(jnp.bfloat16), "vol", scatter_dimension=0, tiled=True
    ).astype(jnp.float32)
    row_panel = lax.psum(partial_rows, "space")
    diag_block = lax.dynamic_slice_in_dim(row_panel, row_start, panel_rows, 1)
    trace_value = lax.psum(jnp.trace(diag_block), "vol")
    normed_panel = row_panel / total_patches
    mean_diagonal = trace_value / total_patches / gram_width
    basis_rows = lax.dynamic_slice_in_dim(basis, row_start, panel_rows, 0)
    product = jnp.dot(
        normed_panel, basis, precision=lax.Precision.HIGHEST, preferred_element_type=jnp.float32
    )
    return product + damping[0] * mean_diagonal * basis_rows


def wait_halo(present, halo_copy, halo):
    @pl.when(present)
    def _():
        halo_copy().wait_recv()

    @pl.when(jnp.logical_not(present))
    def _():
        halo[...] = jnp.zeros_like(halo)


def own_patches(
    cells_ref, weight_ref, bias_ref, halo, weights, taps, partial, active, padded, wait
):
    planes, rows_y, chans, cols_z = cells_ref.shape
    out_rows = [y for y in range(rows_y) if y % 4]
    lane = lax.broadcasted_iota(jnp.int32, (rows_y * chans, cols_z), 1)

    for d in range(3):
        weights[d * chans : (d + 1) * chans] = jnp.concatenate(
            [weight_ref[9 * d + t].astype(jnp.float32) for t in range(9)], axis=1
        ).astype(jnp.bfloat16)

    def plane(p, cells):
        wide = cells.astype(jnp.float32).reshape(rows_y * chans, cols_z)
        left = jnp.where(lane == 0, 0.0, pltpu.roll(wide, 1, 1))
        right = jnp.where(lane == cols_z - 1, 0.0, pltpu.roll(wide, cols_z - 1, 1))
        for d, moved in enumerate((left, wide, right)):
            taps[0:rows_y, d] = moved.astype(jnp.bfloat16).reshape(rows_y, chans, cols_z)
        taps[rows_y] = jnp.zeros_like(taps[rows_y])
        for n, y in enumerate(out_rows):
            window = taps[y - 1 : y + 2].reshape(9 * chans, cols_z)
            partial[p, n] = jnp.dot(
                weights[...], window, preferred_element_type=jnp.float32
            )

    for p in range(planes):
        plane(p, cells_ref[p])

    source = lax.broadcasted_iota(jnp.int32, (9 * chans, padded), 0)
    target = lax.broadcasted_iota(jnp.int32, (9 * chans, padded), 1)
    target -= (source % chans) * 27 + (source // chans) * 3
    order = [jnp.where(target == c, 1.0, 0.0).astype(jnp.bfloat16) for c in range(3)]
    ks = cols_z // 4
    row = lax.broadcasted_iota(jnp.int32, (3 * ks, cols_z), 0)
    col = lax.broadcasted_iota(jnp.int32, (3 * ks, cols_z), 1)
    pick = jnp.where(col == 4 * (row % ks) + row // ks + 1, 1.0, 0.0).astype(jnp.bfloat16)

    square = (chans, chans)
    diagonal = lax.broadcasted_iota(jnp.int32, square, 0) == lax.broadcasted_iota(
        jnp.int32, square, 1
    )
    bias = jnp.sum(jnp.where(diagonal, bias_ref[...], 0.0), axis=1, keepdims=True)

    wait()
    plane(planes, halo[...])

    picked = []
    for j in range(rows_y // 4):
        for a in range(3):
            for b in range(3):
                n = 3 * j + b
                value = partial[a, n, 0:chans] + partial[a + 1, n, chans : 2 * chans]
                value += partial[a + 2, n, 2 * chans : 3 * chans]
                value = jnp.maximum(value + bias, 0.0).astype(jnp.bfloat16)
                active[(3 * a + b) * chans : (3 * a + b + 1) * chans] = value
        picked.append(
            lax.dot_general(
                pick, active[...], (((1,), (1,)), ((), ())), preferred_element_type=jnp.float32
            ).astype(jnp.bfloat16)
        )
    total = None
    for c in range(3):
        part = jnp.concatenate([x[c * ks : (c + 1) * ks] for x in picked], axis=0)
        term = jnp.dot(part, order[c], preferred_element_type=jnp.float32)
        total = term if total is None else total + term
    return total.astype(jnp.bfloat16)


def gather_kernel(
    nz, total, cells_ref, weight_ref, bias_ref, basis_hbm, damping_ref, out_ref,
    halo, weights, taps, partial, active, buf, acc, square, basis_f32, basis_hi, basis_lo,
    basis_sem, halo_send, halo_recv, z_send, x_send, y_send, a_send, b_send, c_send,
    z_recv, x_recv, y_recv, a_recv, b_recv, c_recv,
):
    vol = lax.axis_index("vol")
    space = lax.axis_index("space")
    z = space // 4
    here = (vol, space)
    core_peer = (vol, space + 1 - 2 * lax.rem(space, 2))
    x_peer = (vol, space + 2 - 4 * lax.rem(space // 2, 2))
    y_peer = (1 - vol, space)
    up_peer, down_peer = (vol, space + 4), (vol, space - 4)
    patches, padded = buf.shape[3:]
    ends = lax.axis_size("space")
    half = patches // 2
    panel, width = out_ref.shape

    basis_copy = pltpu.make_async_copy(basis_hbm, basis_f32, basis_sem)
    basis_copy.start()

    barrier = pltpu.get_barrier_semaphore()
    for peer in (core_peer, x_peer, y_peer):
        pl.semaphore_signal(barrier, inc=1, device_id=peer, device_id_type=MESH)

    @pl.when(z + 1 < nz)
    def _():
        pl.semaphore_signal(barrier, inc=1, device_id=up_peer, device_id_type=MESH)

    @pl.when(z > 0)
    def _():
        pl.semaphore_signal(barrier, inc=1, device_id=down_peer, device_id_type=MESH)

    @pl.when(space > 0)
    def _():
        pl.semaphore_signal(barrier, inc=1, device_id=(vol, space - 1), device_id_type=MESH)

    @pl.when(space + 1 < ends)
    def _():
        pl.semaphore_signal(barrier, inc=1, device_id=(vol, space + 1), device_id_type=MESH)

    edges = jnp.where(z > 0, 1, 0) + jnp.where(z + 1 < nz, 1, 0)
    edges += jnp.where(space > 0, 1, 0) + jnp.where(space + 1 < ends, 1, 0)
    pl.semaphore_wait(barrier, 3 + edges)

    def remote(src, dst, send, recv, peer):
        return pltpu.make_async_remote_copy(
            src_ref=src, dst_ref=dst, send_sem=send, recv_sem=recv,
            device_id=peer, device_id_type=MESH,
        )

    def halo_copy():
        return remote(cells_ref.at[0], halo, halo_send, halo_recv, (vol, space - 1))

    pl.when(space > 0)(lambda: halo_copy().start())
    buf[0, 0, z] = own_patches(
        cells_ref, weight_ref, bias_ref, halo, weights, taps, partial, active, padded,
        lambda: wait_halo(space + 1 < ends, halo_copy, halo),
    )

    def z_copy(k, peer, way):
        return remote(buf.at[0, 0, k], buf.at[0, 0, k], z_send.at[way, k], z_recv.at[k], peer)

    def x_copy(k):
        return remote(buf.at[0, 0, k], buf.at[0, 1, k], x_send.at[k], x_recv.at[k], x_peer)

    def y_copy(k):
        return remote(buf.at[0, 0, k], buf.at[0, 2, k], y_send.at[k], y_recv.at[k], y_peer)

    def a_copy(k):
        rows = pl.ds(0, half)
        return remote(
            buf.at[0, 1, k, rows], buf.at[0, 3, k, rows], a_send.at[k], a_recv.at[k], y_peer
        )

    def b_copy(k):
        rows = pl.ds(half, half)
        return remote(
            buf.at[0, 2, k, rows], buf.at[0, 3, k, rows], b_send.at[k], b_recv.at[k], x_peer
        )

    def c_copy(q, k):
        return remote(
            buf.at[0, q, k], buf.at[1, q, k], c_send.at[q, k], c_recv.at[q, k], core_peer
        )

    def spread(k):
        x_copy(k).start()
        y_copy(k).start()
        c_copy(0, k).start()

    def relay(k):
        x_copy(k).wait_recv()
        a_copy(k).start()
        c_copy(1, k).start()
        y_copy(k).wait_recv()
        b_copy(k).start()
        c_copy(2, k).start()

    def finish(k):
        a_copy(k).wait_recv()
        b_copy(k).wait_recv()
        c_copy(3, k).start()

    def both(s, action):
        if s == 0:
            action(z)
            return
        pl.when(z >= s)(lambda: action(z - s))
        pl.when(z + s < nz)(lambda: action(z + s))

    def gram(c, q):
        block = buf[c, q].reshape(nz * patches, padded)
        turned = block.T
        wide = block.astype(jnp.float32)
        sums = jnp.sum((wide * wide).reshape(-1, 8, padded), axis=0)
        rows = jnp.where(vol == 0, turned[:panel], turned[panel : 2 * panel])
        term = jnp.dot(rows, block, preferred_element_type=jnp.float32)
        if c == 0 and q == 0:
            acc[...] = term
            square[...] = sums
        else:
            acc[...] += term
            square[...] += sums

    pl.when(z + 1 < nz)(lambda: z_copy(z, up_peer, 0).start())
    pl.when(z > 0)(lambda: z_copy(z, down_peer, 1).start())
    spread(z)

    basis_copy.wait()
    basis_hi[...] = basis_f32[...].astype(jnp.bfloat16)
    basis_lo[...] = (basis_f32[...] - basis_hi[...].astype(jnp.float32)).astype(jnp.bfloat16)

    for s in range(1, nz):
        @pl.when(z >= s)
        def _():
            k = z - s
            z_copy(k, up_peer, 0).wait_recv()
            pl.when(z + 1 < nz)(lambda: z_copy(k, up_peer, 0).start())
            spread(k)

        @pl.when(z + s < nz)
        def _():
            k = z + s
            z_copy(k, down_peer, 1).wait_recv()
            pl.when(z > 0)(lambda: z_copy(k, down_peer, 1).start())
            spread(k)

        both(s - 1, relay)
    both(nz - 1, relay)

    def other_core(q):
        for k in range(nz):
            c_copy(q, k).wait_recv()
        gram(1, q)

    early = [
        lambda: gram(0, 0), lambda: other_core(0), lambda: gram(0, 1),
        lambda: gram(0, 2), lambda: other_core(1), lambda: other_core(2),
    ]
    for s in range(nz):
        share = -(-len(early) // (nz - s))
        for step in early[:share]:
            step()
        early = early[share:]
        both(s, finish)
    gram(0, 3)
    other_core(3)

    scale = 1.0 / total
    mean_diag = jnp.sum(square[...]) * (scale / width)
    value = acc[:, :width]
    high = value.astype(jnp.bfloat16)
    low = (value - high.astype(jnp.float32)).astype(jnp.bfloat16)
    product = jnp.dot(high, basis_hi[...], preferred_element_type=jnp.float32)
    product += jnp.dot(high, basis_lo[...], preferred_element_type=jnp.float32)
    product += jnp.dot(low, basis_hi[...], preferred_element_type=jnp.float32)
    basis_rows = basis_f32[pl.ds(pl.multiple_of(vol * panel, 16), panel), :]
    out_ref[...] = product * scale + (damping_ref[0] * mean_diag) * basis_rows

    pl.when(space > 0)(lambda: halo_copy().wait_send())
    for k in range(nz):
        pl.when((z + 1 < nz) & (k <= z))(lambda: z_copy(k, up_peer, 0).wait_send())
        pl.when((z > 0) & (k >= z))(lambda: z_copy(k, down_peer, 1).wait_send())
        x_copy(k).wait_send()
        y_copy(k).wait_send()
        a_copy(k).wait_send()
        b_copy(k).wait_send()
        for q in range(4):
            c_copy(q, k).wait_send()


def body_gather(volume, conv_weight, conv_bias, basis, damping):
    chans, planes, rows_y, cols_z = volume.shape[1:]
    width = chans * 27
    patches = (planes // 4) * (rows_y // 4) * (cols_z // 4)
    cells = volume[0].transpose(1, 2, 0, 3)
    weight = conv_weight.transpose(2, 3, 4, 0, 1).reshape(27, chans, chans)
    padded = -(-width // 128) * 128
    space = lax.axis_size("space")
    nz = space // 4
    panel = width // lax.axis_size("vol")
    total = patches * space * lax.axis_size("vol")
    dma = pltpu.SemaphoreType.DMA
    return pl.pallas_call(
        functools.partial(gather_kernel, nz, total),
        out_shape=jax.ShapeDtypeStruct((panel, width), jnp.float32),
        in_specs=[
            pl.BlockSpec(memory_space=pltpu.VMEM),
            pl.BlockSpec(memory_space=pltpu.VMEM),
            pl.BlockSpec(memory_space=pltpu.VMEM),
            pl.BlockSpec(memory_space=pltpu.HBM),
            pl.BlockSpec(memory_space=pltpu.SMEM),
        ],
        out_specs=pl.BlockSpec(memory_space=pltpu.VMEM),
        scratch_shapes=[
            pltpu.VMEM((rows_y, chans, cols_z), jnp.bfloat16),
            pltpu.VMEM((3 * chans, 9 * chans), jnp.bfloat16),
            pltpu.VMEM((rows_y + 1, 3, chans, cols_z), jnp.bfloat16),
            pltpu.VMEM((planes + 1, 3 * rows_y // 4, 3 * chans, cols_z), jnp.float32),
            pltpu.VMEM((9 * chans, cols_z), jnp.bfloat16),
            pltpu.VMEM((2, 4, nz, patches, padded), jnp.bfloat16),
            pltpu.VMEM((panel, padded), jnp.float32),
            pltpu.VMEM((8, padded), jnp.float32),
            pltpu.VMEM((width, width), jnp.float32),
            pltpu.VMEM((width, width), jnp.bfloat16),
            pltpu.VMEM((width, width), jnp.bfloat16),
            dma, dma, dma,
            dma((2, nz)), dma((nz,)), dma((nz,)), dma((nz,)), dma((nz,)), dma((4, nz)),
            dma((nz,)), dma((nz,)), dma((nz,)), dma((nz,)), dma((nz,)), dma((4, nz)),
        ],
        compiler_params=pltpu.CompilerParams(
            collective_id=0, has_side_effects=True, vmem_limit_bytes=51 << 20
        ),
    )(cells, weight, conv_bias[None, :], basis, damping)


def body(volume, conv_weight, conv_bias, basis, damping):
    vol, space = lax.axis_size("vol"), lax.axis_size("space")
    cells = volume.shape[2] * volume.shape[3] * volume.shape[4]
    gathered = 2 * volume.shape[1] * 27 * (cells // 64) * vol * space
    one_plane = volume.shape[2] == 4 and volume.shape[4] % 128 == 0
    if one_plane and vol == 2 and space % 4 == 0 and gathered <= GATHER_LIMIT:
        return body_gather(volume, conv_weight, conv_bias, basis, damping)
    return body_collective(volume, conv_weight, conv_bias, basis, damping)


def solution(mesh):
    in_specs = (P("vol", None, "space", None, None), P(), P(), P(), P())
    out_specs = P("vol", None)
    return jax.shard_map(body, mesh=mesh, in_specs=in_specs, out_specs=out_specs, check_vma=False)
```

```python
import functools

import jax
import jax.numpy as jnp
from jax import lax
from jax.experimental import pallas as pl
from jax.experimental.pallas import tpu as pltpu
from jax.sharding import PartitionSpec as P

MESH = pl.DeviceIdType.MESH
GATHER_LIMIT = 8 << 20


def shifted(block, axis, distance):
    devices = range(lax.axis_size(axis))
    route = [(i - distance, i) for i in devices if i - distance in devices]
    return lax.ppermute(block, axis, route)


def split_patches(activated):
    chans, planes, rows_y, cols_z = activated.shape
    return activated.reshape(chans, planes // 4, 4, rows_y // 4, 4, cols_z // 4, 4)[
        :, :, 1:, :, 1:, :, 1:
    ]


def conv_block(volume, conv_weight, conv_bias):
    local_block = volume[0]
    from_above = shifted(local_block[:, 0:1], "space", -1)
    zero_plane = jnp.zeros_like(from_above)
    stacked = jnp.concatenate([zero_plane, local_block, from_above], axis=1)
    conv_out = lax.conv_general_dilated(
        stacked[None],
        conv_weight,
        (1, 1, 1),
        [(0, 0), (1, 1), (1, 1)],
        dimension_numbers=("NCDHW", "OIDHW", "NCDHW"),
        preferred_element_type=jnp.float32,
    )[0]
    return jnp.maximum(conv_out + conv_bias[:, None, None, None], 0.0).astype(jnp.bfloat16)


def body_collective(volume, conv_weight, conv_bias, basis, damping):
    viewed = split_patches(conv_block(volume, conv_weight, conv_bias))
    patch_cols = viewed.transpose(0, 2, 4, 6, 1, 3, 5).reshape(viewed.shape[0] * 27, -1)
    local_gram = jnp.dot(patch_cols, patch_cols.T, preferred_element_type=jnp.float32)
    gram_width = local_gram.shape[0]
    total_patches = patch_cols.shape[1] * lax.axis_size("space") * lax.axis_size("vol")
    panel_rows = gram_width // lax.axis_size("vol")
    row_start = lax.axis_index("vol") * panel_rows
    partial_rows = lax.psum_scatter(
        local_gram.astype(jnp.bfloat16), "vol", scatter_dimension=0, tiled=True
    ).astype(jnp.float32)
    row_panel = lax.psum(partial_rows, "space")
    diag_block = lax.dynamic_slice_in_dim(row_panel, row_start, panel_rows, 1)
    trace_value = lax.psum(jnp.trace(diag_block), "vol")
    normed_panel = row_panel / total_patches
    mean_diagonal = trace_value / total_patches / gram_width
    basis_rows = lax.dynamic_slice_in_dim(basis, row_start, panel_rows, 0)
    product = jnp.dot(
        normed_panel, basis, precision=lax.Precision.HIGHEST, preferred_element_type=jnp.float32
    )
    return product + damping[0] * mean_diagonal * basis_rows


def wait_halo(present, halo_copy, halo):
    @pl.when(present)
    def _():
        halo_copy().wait_recv()

    @pl.when(jnp.logical_not(present))
    def _():
        halo[...] = jnp.zeros_like(halo)


def own_patches(
    cells_ref, weight_ref, bias_ref, halo, weights, taps, partial, active, padded, wait
):
    planes, rows_y, chans, cols_z = cells_ref.shape
    out_rows = [y for y in range(rows_y) if y % 4]
    lane = lax.broadcasted_iota(jnp.int32, (rows_y * chans, cols_z), 1)

    for d in range(3):
        weights[d * chans : (d + 1) * chans] = jnp.concatenate(
            [weight_ref[9 * d + t].astype(jnp.float32) for t in range(9)], axis=1
        ).astype(jnp.bfloat16)

    def plane(p, cells):
        wide = cells.astype(jnp.float32).reshape(rows_y * chans, cols_z)
        left = jnp.where(lane == 0, 0.0, pltpu.roll(wide, 1, 1))
        right = jnp.where(lane == cols_z - 1, 0.0, pltpu.roll(wide, cols_z - 1, 1))
        for d, moved in enumerate((left, wide, right)):
            taps[0:rows_y, d] = moved.astype(jnp.bfloat16).reshape(rows_y, chans, cols_z)
        taps[rows_y] = jnp.zeros_like(taps[rows_y])
        for n, y in enumerate(out_rows):
            window = taps[y - 1 : y + 2].reshape(9 * chans, cols_z)
            partial[p, n] = jnp.dot(
                weights[...], window, preferred_element_type=jnp.float32
            )

    for p in range(planes):
        plane(p, cells_ref[p])

    source = lax.broadcasted_iota(jnp.int32, (9 * chans, padded), 0)
    target = lax.broadcasted_iota(jnp.int32, (9 * chans, padded), 1)
    target -= (source % chans) * 27 + (source // chans) * 3
    order = [jnp.where(target == c, 1.0, 0.0).astype(jnp.bfloat16) for c in range(3)]
    ks = cols_z // 4
    row = lax.broadcasted_iota(jnp.int32, (3 * ks, cols_z), 0)
    col = lax.broadcasted_iota(jnp.int32, (3 * ks, cols_z), 1)
    pick = jnp.where(col == 4 * (row % ks) + row // ks + 1, 1.0, 0.0).astype(jnp.bfloat16)

    square = (chans, chans)
    diagonal = lax.broadcasted_iota(jnp.int32, square, 0) == lax.broadcasted_iota(
        jnp.int32, square, 1
    )
    bias = jnp.sum(jnp.where(diagonal, bias_ref[...], 0.0), axis=1, keepdims=True)

    wait()
    plane(planes, halo[...])

    picked = []
    for j in range(rows_y // 4):
        for a in range(3):
            for b in range(3):
                n = 3 * j + b
                value = partial[a, n, 0:chans] + partial[a + 1, n, chans : 2 * chans]
                value += partial[a + 2, n, 2 * chans : 3 * chans]
                value = jnp.maximum(value + bias, 0.0).astype(jnp.bfloat16)
                active[(3 * a + b) * chans : (3 * a + b + 1) * chans] = value
        picked.append(
            lax.dot_general(
                pick, active[...], (((1,), (1,)), ((), ())), preferred_element_type=jnp.float32
            ).astype(jnp.bfloat16)
        )
    total = None
    for c in range(3):
        part = jnp.concatenate([x[c * ks : (c + 1) * ks] for x in picked], axis=0)
        term = jnp.dot(part, order[c], preferred_element_type=jnp.float32)
        total = term if total is None else total + term
    return total.astype(jnp.bfloat16)


def gather_kernel(
    nz, total, cells_ref, weight_ref, bias_ref, basis_hbm, damping_ref, out_ref,
    halo, weights, taps, partial, active, buf, acc, square, basis_f32, basis_hi, basis_lo,
    basis_sem, halo_send, halo_recv, z_send, x_send, y_send, a_send, b_send, c_send, d_send,
    z_recv, x_recv, y_recv, a_recv, b_recv, c_recv, d_recv,
):
    vol = lax.axis_index("vol")
    space = lax.axis_index("space")
    z = space // 4
    here = (vol, space)
    core_peer = (vol, space + 1 - 2 * lax.rem(space, 2))
    x_peer = (vol, space + 2 - 4 * lax.rem(space // 2, 2))
    y_peer = (1 - vol, space)
    up_peer, down_peer = (vol, space + 4), (vol, space - 4)
    patches, padded = buf.shape[3:]
    ends = lax.axis_size("space")
    half = patches // 2
    panel, width = out_ref.shape

    basis_copy = pltpu.make_async_copy(basis_hbm, basis_f32, basis_sem)
    basis_copy.start()

    barrier = pltpu.get_barrier_semaphore()
    for peer in (core_peer, x_peer, y_peer):
        pl.semaphore_signal(barrier, inc=1, device_id=peer, device_id_type=MESH)

    @pl.when(z + 1 < nz)
    def _():
        pl.semaphore_signal(barrier, inc=1, device_id=up_peer, device_id_type=MESH)

    @pl.when(z > 0)
    def _():
        pl.semaphore_signal(barrier, inc=1, device_id=down_peer, device_id_type=MESH)

    @pl.when(space > 0)
    def _():
        pl.semaphore_signal(barrier, inc=1, device_id=(vol, space - 1), device_id_type=MESH)

    @pl.when(space + 1 < ends)
    def _():
        pl.semaphore_signal(barrier, inc=1, device_id=(vol, space + 1), device_id_type=MESH)

    edges = jnp.where(z > 0, 1, 0) + jnp.where(z + 1 < nz, 1, 0)
    edges += jnp.where(space > 0, 1, 0) + jnp.where(space + 1 < ends, 1, 0)
    pl.semaphore_wait(barrier, 3 + edges)

    def remote(src, dst, send, recv, peer):
        return pltpu.make_async_remote_copy(
            src_ref=src, dst_ref=dst, send_sem=send, recv_sem=recv,
            device_id=peer, device_id_type=MESH,
        )

    def halo_copy():
        return remote(cells_ref.at[0], halo, halo_send, halo_recv, (vol, space - 1))

    pl.when(space > 0)(lambda: halo_copy().start())
    buf[0, 0, z] = own_patches(
        cells_ref, weight_ref, bias_ref, halo, weights, taps, partial, active, padded,
        lambda: wait_halo(space + 1 < ends, halo_copy, halo),
    )

    def z_copy(k, peer, way):
        return remote(buf.at[0, 0, k], buf.at[0, 0, k], z_send.at[way, k], z_recv.at[k], peer)

    def x_copy(k):
        return remote(buf.at[0, 0, k], buf.at[0, 1, k], x_send.at[k], x_recv.at[k], x_peer)

    def y_copy(k):
        return remote(buf.at[0, 0, k], buf.at[0, 2, k], y_send.at[k], y_recv.at[k], y_peer)

    def a_copy(k):
        rows = pl.ds(0, half)
        return remote(
            buf.at[0, 1, k, rows], buf.at[0, 3, k, rows], a_send.at[k], a_recv.at[k], y_peer
        )

    def b_copy(k):
        rows = pl.ds(half, half)
        return remote(
            buf.at[0, 2, k, rows], buf.at[0, 3, k, rows], b_send.at[k], b_recv.at[k], x_peer
        )

    def d_copy(k, peer, way):
        return remote(buf.at[0, 3, k], buf.at[0, 3, k], d_send.at[way, k], d_recv.at[k], peer)

    def c_copy(q, k):
        return remote(
            buf.at[0, q, k], buf.at[1, q, k], c_send.at[q, k], c_recv.at[q, k], core_peer
        )

    def spread(k):
        x_copy(k).start()
        y_copy(k).start()
        c_copy(0, k).start()

    def relay(k, s):
        x_copy(k).wait_recv()
        if s <= 1:
            a_copy(k).start()
        c_copy(1, k).start()
        y_copy(k).wait_recv()
        if s <= 1:
            b_copy(k).start()
        c_copy(2, k).start()

    def finish(k, s):
        if s <= 1:
            a_copy(k).wait_recv()
            b_copy(k).wait_recv()
        else:
            d_copy(k, up_peer, 0).wait_recv()
        if s >= 1:
            pl.when((k < z) & (z + 1 < nz))(lambda: d_copy(k, up_peer, 0).start())
            pl.when((k > z) & (z > 0))(lambda: d_copy(k, down_peer, 1).start())
        c_copy(3, k).start()

    def both(s, action):
        if s == 0:
            action(z, s)
            return
        pl.when(z >= s)(lambda: action(z - s, s))
        pl.when(z + s < nz)(lambda: action(z + s, s))

    def gram(c, q):
        block = buf[c, q].reshape(nz * patches, padded)
        turned = block.T
        wide = block.astype(jnp.float32)
        sums = jnp.sum((wide * wide).reshape(-1, 8, padded), axis=0)
        rows = jnp.where(vol == 0, turned[:panel], turned[panel : 2 * panel])
        term = jnp.dot(rows, block, preferred_element_type=jnp.float32)
        if c == 0 and q == 0:
            acc[...] = term
            square[...] = sums
        else:
            acc[...] += term
            square[...] += sums

    pl.when(z + 1 < nz)(lambda: z_copy(z, up_peer, 0).start())
    pl.when(z > 0)(lambda: z_copy(z, down_peer, 1).start())
    spread(z)

    basis_copy.wait()
    basis_hi[...] = basis_f32[...].astype(jnp.bfloat16)
    basis_lo[...] = (basis_f32[...] - basis_hi[...].astype(jnp.float32)).astype(jnp.bfloat16)

    for s in range(1, nz):
        @pl.when(z >= s)
        def _():
            k = z - s
            z_copy(k, up_peer, 0).wait_recv()
            pl.when(z + 1 < nz)(lambda: z_copy(k, up_peer, 0).start())
            spread(k)

        @pl.when(z + s < nz)
        def _():
            k = z + s
            z_copy(k, down_peer, 1).wait_recv()
            pl.when(z > 0)(lambda: z_copy(k, down_peer, 1).start())
            spread(k)

        both(s - 1, relay)
    both(nz - 1, relay)

    def other_core(q):
        for k in range(nz):
            c_copy(q, k).wait_recv()
        gram(1, q)

    early = [
        lambda: gram(0, 0), lambda: other_core(0), lambda: gram(0, 1),
        lambda: gram(0, 2), lambda: other_core(1), lambda: other_core(2),
    ]
    for s in range(nz):
        share = -(-len(early) // (nz - s))
        for step in early[:share]:
            step()
        early = early[share:]
        both(s, finish)
    gram(0, 3)
    other_core(3)

    scale = 1.0 / total
    mean_diag = jnp.sum(square[...]) * (scale / width)
    value = acc[:, :width]
    high = value.astype(jnp.bfloat16)
    low = (value - high.astype(jnp.float32)).astype(jnp.bfloat16)
    product = jnp.dot(high, basis_hi[...], preferred_element_type=jnp.float32)
    product += jnp.dot(high, basis_lo[...], preferred_element_type=jnp.float32)
    product += jnp.dot(low, basis_hi[...], preferred_element_type=jnp.float32)
    basis_rows = basis_f32[pl.ds(pl.multiple_of(vol * panel, 16), panel), :]
    out_ref[...] = product * scale + (damping_ref[0] * mean_diag) * basis_rows

    pl.when(space > 0)(lambda: halo_copy().wait_send())
    for k in range(nz):
        pl.when((z + 1 < nz) & (k <= z))(lambda: z_copy(k, up_peer, 0).wait_send())
        pl.when((z > 0) & (k >= z))(lambda: z_copy(k, down_peer, 1).wait_send())
        x_copy(k).wait_send()
        y_copy(k).wait_send()
        @pl.when((z - k <= 1) & (k - z <= 1))
        def _():
            a_copy(k).wait_send()
            b_copy(k).wait_send()

        pl.when((z + 1 < nz) & (k < z))(lambda: d_copy(k, up_peer, 0).wait_send())
        pl.when((z > 0) & (k > z))(lambda: d_copy(k, down_peer, 1).wait_send())
        for q in range(4):
            c_copy(q, k).wait_send()


def body_gather(volume, conv_weight, conv_bias, basis, damping):
    chans, planes, rows_y, cols_z = volume.shape[1:]
    width = chans * 27
    patches = (planes // 4) * (rows_y // 4) * (cols_z // 4)
    cells = volume[0].transpose(1, 2, 0, 3)
    weight = conv_weight.transpose(2, 3, 4, 0, 1).reshape(27, chans, chans)
    padded = -(-width // 128) * 128
    space = lax.axis_size("space")
    nz = space // 4
    panel = width // lax.axis_size("vol")
    total = patches * space * lax.axis_size("vol")
    dma = pltpu.SemaphoreType.DMA
    return pl.pallas_call(
        functools.partial(gather_kernel, nz, total),
        out_shape=jax.ShapeDtypeStruct((panel, width), jnp.float32),
        in_specs=[
            pl.BlockSpec(memory_space=pltpu.VMEM),
            pl.BlockSpec(memory_space=pltpu.VMEM),
            pl.BlockSpec(memory_space=pltpu.VMEM),
            pl.BlockSpec(memory_space=pltpu.HBM),
            pl.BlockSpec(memory_space=pltpu.SMEM),
        ],
        out_specs=pl.BlockSpec(memory_space=pltpu.VMEM),
        scratch_shapes=[
            pltpu.VMEM((rows_y, chans, cols_z), jnp.bfloat16),
            pltpu.VMEM((3 * chans, 9 * chans), jnp.bfloat16),
            pltpu.VMEM((rows_y + 1, 3, chans, cols_z), jnp.bfloat16),
            pltpu.VMEM((planes + 1, 3 * rows_y // 4, 3 * chans, cols_z), jnp.float32),
            pltpu.VMEM((9 * chans, cols_z), jnp.bfloat16),
            pltpu.VMEM((2, 4, nz, patches, padded), jnp.bfloat16),
            pltpu.VMEM((panel, padded), jnp.float32),
            pltpu.VMEM((8, padded), jnp.float32),
            pltpu.VMEM((width, width), jnp.float32),
            pltpu.VMEM((width, width), jnp.bfloat16),
            pltpu.VMEM((width, width), jnp.bfloat16),
            dma, dma, dma,
            dma((2, nz)), dma((nz,)), dma((nz,)), dma((nz,)), dma((nz,)), dma((4, nz)), dma((2, nz)),
            dma((nz,)), dma((nz,)), dma((nz,)), dma((nz,)), dma((nz,)), dma((4, nz)), dma((nz,)),
        ],
        compiler_params=pltpu.CompilerParams(
            collective_id=0, has_side_effects=True, vmem_limit_bytes=51 << 20
        ),
    )(cells, weight, conv_bias[None, :], basis, damping)


def body(volume, conv_weight, conv_bias, basis, damping):
    vol, space = lax.axis_size("vol"), lax.axis_size("space")
    cells = volume.shape[2] * volume.shape[3] * volume.shape[4]
    gathered = 2 * volume.shape[1] * 27 * (cells // 64) * vol * space
    one_plane = volume.shape[2] == 4 and volume.shape[4] % 128 == 0
    if one_plane and vol == 2 and space % 4 == 0 and gathered <= GATHER_LIMIT:
        return body_gather(volume, conv_weight, conv_bias, basis, damping)
    return body_collective(volume, conv_weight, conv_bias, basis, damping)


def solution(mesh):
    in_specs = (P("vol", None, "space", None, None), P(), P(), P(), P())
    out_specs = P("vol", None)
    return jax.shard_map(body, mesh=mesh, in_specs=in_specs, out_specs=out_specs, check_vma=False)
```
